256 devices in a mesh: ctx: 16 (over z, x_lo), wt: 4 (over x_hi, core), head: 4 (over y).
Axes of the slice: x: 4 (x_hi: 2, x_lo: 2; x = x_hi * 2 + x_lo), y: 4, z: 8, core: 2. Of those that a mesh axis runs over, the one named last changes fastest.
Arguments:
- query_compressed: bfloat16 [2, 1024, 1536], P(None, 'ctx', 'wt'), may hold values from -6 to 6
- query_gain: float32 [1536], replicated, may hold values from 0.25 to 1.75
- w_query: bfloat16 [1536, 24576], P(None, ('wt', 'head')), may hold values from -0.15625 to 0.15625
- new_latent: bfloat16 [2, 1024, 576], P(None, 'ctx'), may hold values from -6 to 6
- latent_gain: float32 [512], replicated, may hold values from 0.25 to 1.75
- cache: bfloat16 [2, 4096, 576], P(None, 'ctx'), may hold values from -1100 to 1100
- prefix_len: int32 [2], replicated, may hold values from 1024 to 4096, as said below
- w_key_up: bfloat16 [128, 512, 128], P(('wt', 'head'), 'ctx'), may hold values from -0.5 to 0.5
- w_value_up: bfloat16 [128, 512, 128], P(('wt', 'head'), 'ctx'), may hold values from -4 to 4
Outputs:
- attended: bfloat16 [2, 1024, 16384], P(None, 'ctx', ('wt', 'head'))
The draws below stay inside these ranges and needn't reach their ends.
Inputs may be any that keep to these rules, and one draw needn't show every extreme that they name: `prefix_len`: one prompt's prefix fills all 4096 cache slots.
All inputs are finite; a program needn't handle non-finite values.
Results may differ from the reference program's by a relative error of at most 0.029.
Values may be sent and summed in bfloat16 or wider, within the bound.
A program may use at most 128 MiB of HBM per device.

```python
import jax
import jax.numpy as jnp
from jax import lax

H = 128
QL = 1536
KVL = 512
NOPE = 128
ROPE = 64
VH = 128
SEQS = 2
FRESH = 1024
CACHE = 4096


def draw_cache(key, part):
    key = jax.random.fold_in(key, 5)
    base_key = jax.random.fold_in(key, 0)
    shape = (SEQS, CACHE, KVL + ROPE)
    values = jnp.clip(jax.random.normal(base_key, shape, jnp.float32), -6.0, 6.0)
    return values.astype(jnp.bfloat16)


def draw_prefix_len(key, part):
    key = jax.random.fold_in(key, 11)
    length_key, full_key = jax.random.split(key)
    lengths = jax.random.randint(length_key, (SEQS,), CACHE // 4, CACHE)
    filled = jax.random.randint(full_key, (), 0, SEQS)
    return jnp.where(jnp.arange(SEQS) == filled, CACHE, lengths).astype(jnp.int32)


def levels(key, shape, cuts, low, high):
    loudness = 1.0
    for position, blocks in cuts:
        steps = jax.random.uniform(jax.random.fold_in(jax.random.fold_in(key, 6), position), (blocks,), jnp.float32, low / len(cuts), high / len(cuts))
        loudness = loudness * jnp.repeat(jnp.exp(steps), shape[position] // blocks).reshape((-1,) + (1,) * (len(shape) - 1 - position))
    return loudness


def normal_values(stream_key, dims, spread, most, cuts=(), kind=jnp.bfloat16):
    loudness = levels(stream_key, dims, cuts, -0.22, 0.18) if cuts else 1.0
    drawn = jax.random.normal(stream_key, dims, jnp.float32) * spread * loudness
    return jnp.minimum(jnp.maximum(drawn, -most), most).astype(kind)


def setup_inputs(seed: int = 0) -> dict:
    key_list = jax.random.split(jax.random.key(seed), 10)
    return {
        "query_compressed": normal_values(key_list[0], (SEQS, FRESH, QL), 1.0, 6.0, ((1, 16), (2, 4))),
        "query_gain": jnp.clip(1.0 + 0.15 * jax.random.normal(key_list[1], (QL,), jnp.float32), 0.25, 1.75),
        "w_query": normal_values(key_list[2], (QL, H * (NOPE + ROPE)), QL ** -0.5, 0.15625, ((1, 16),)),
        "new_latent": normal_values(key_list[3], (SEQS, FRESH, KVL + ROPE), 1.0, 6.0, ((1, 16),)),
        "latent_gain": jnp.clip(1.0 + 0.15 * jax.random.normal(key_list[4], (KVL,), jnp.float32), 0.25, 1.75),
        "cache": draw_cache(jax.random.fold_in(key_list[9], 71), 0),
        "prefix_len": draw_prefix_len(jax.random.fold_in(key_list[9], 71), 0),
        "w_key_up": normal_values(key_list[7], (H, KVL, NOPE), NOPE ** -0.5, 0.5, ((0, 16), (1, 16))),
        "w_value_up": normal_values(key_list[8], (H, KVL, VH), 2 ** -0.5, 4.0, ((0, 16), (1, 16))),
    }


eps = 1e-06
rope_base = 10000.0

def rms_scale(values, gain_vector):
    mean_square = lax.optimization_barrier(jnp.mean(values * values, axis=-1, keepdims=True))
    return values * lax.rsqrt(mean_square + eps) * gain_vector

def rotate(values, positions):
    half_width = values.shape[-1] // 2
    exponent = jnp.arange(half_width, dtype=jnp.float32) * (-2.0 / values.shape[-1])
    frequency = jnp.exp(exponent * jnp.log(jnp.float32(rope_base)))
    angles = positions[..., None] * frequency
    cosine = jnp.cos(angles)
    sine_values = jnp.sin(angles)
    leading = values[..., :half_width]
    trailing = values[..., half_width:]
    return jnp.concatenate([leading * cosine - trailing * sine_values, trailing * cosine + leading * sine_values], -1)

def reference(query_compressed, query_gain, w_query, new_latent, latent_gain, cache, prefix_len, w_key_up, w_value_up):
    prompts = new_latent.shape[0]
    new_count = new_latent.shape[1]
    head_count = w_key_up.shape[0]
    head_width = w_query.shape[1] // head_count
    tokens = jnp.arange(new_count, dtype=jnp.int32)
    positions = (prefix_len[:, None] + tokens[None, :]).astype(jnp.float32)
    q_normed = rms_scale(query_compressed.astype(jnp.float32), query_gain).astype(jnp.bfloat16)
    q_full = jnp.dot(q_normed.reshape(prompts * new_count, -1), w_query, preferred_element_type=jnp.float32)
    q_full = q_full.reshape(prompts, new_count, head_count, head_width)
    q_nope = q_full[..., :NOPE].astype(jnp.bfloat16)
    q_rope = rotate(jnp.swapaxes(q_full[..., NOPE:], 1, 2), positions[:, None, :]).astype(jnp.bfloat16)
    latent_part = rms_scale(new_latent[..., :KVL].astype(jnp.float32), latent_gain).astype(jnp.bfloat16)
    rope_part = rotate(new_latent[..., KVL:].astype(jnp.float32), positions).astype(jnp.bfloat16)
    key_rows = jnp.concatenate([cache, jnp.concatenate([latent_part, rope_part], -1)], 1).astype(jnp.float32)
    slot_index = jnp.arange(CACHE + new_count, dtype=jnp.int32)
    cache_ok = (slot_index[None, :] < prefix_len[:, None]) & (slot_index[None, :] < CACHE)
    fresh_ok = (slot_index[None, :] >= CACHE) & (slot_index[None, :] - CACHE <= tokens[:, None])
    visible = cache_ok[:, None, :] | fresh_ok[None, :, :]
    score_scale = (NOPE + ROPE) ** (-0.5)

    def one_head(inputs):
        nope_head, rope_head, key_up, value_up = inputs
        q_lat = jnp.einsum('scd,kd->sck', nope_head.astype(jnp.float32), key_up.astype(jnp.float32)).astype(jnp.bfloat16)
        scores = jnp.einsum('sck,snk->scn', q_lat.astype(jnp.float32), key_rows[..., :KVL])
        scores = scores + jnp.einsum('scr,snr->scn', rope_head.astype(jnp.float32), key_rows[..., KVL:])
        scores = jnp.where(visible, scores * score_scale, -1e+30)
        row_max = lax.optimization_barrier(jnp.max(scores, axis=-1, keepdims=True))
        weights = jnp.where(visible, jnp.exp(scores - row_max), 0.0)
        weight_sum = lax.optimization_barrier(jnp.sum(weights, axis=-1, keepdims=True))
        rounded = weights.astype(jnp.bfloat16).astype(jnp.float32)
        o_lat = (jnp.einsum('scn,snk->sck', rounded, key_rows[..., :KVL]) / weight_sum).astype(jnp.bfloat16)
        return jnp.einsum('sck,kv->scv', o_lat.astype(jnp.float32), value_up.astype(jnp.float32)).astype(jnp.bfloat16)
    per_head = lax.map(one_head, (jnp.moveaxis(q_nope, 2, 0), jnp.moveaxis(q_rope, 1, 0), w_key_up, w_value_up))
    return jnp.moveaxis(per_head, 0, 2).reshape(prompts, new_count, head_count * VH)
```

```python
import jax
import jax.numpy as jnp
from jax import lax
from jax.experimental import pallas as pl
from jax.experimental.pallas import tpu as pltpu
from jax.sharding import PartitionSpec as P

MESH = pl.DeviceIdType.MESH
eps = 1e-06
rope_base = 10000.0
SLICE = 80
CUT = 48
KEYS = 8 * SLICE
NEG = -1e30
SCALE = 1.4426950408889634 * (192 ** -0.5)
ORDER = [0, -1, 1, -2, 2, -3, 3, 4]
DY = [0, -1, 1, 2]


def remote(src, dst, send_sem, recv_sem, device):
    return pltpu.make_async_remote_copy(
        src_ref=src, dst_ref=dst, send_sem=send_sem, recv_sem=recv_sem, device_id=device, device_id_type=MESH
    )


def kernel(
    qc_ref, gain_ref, wq_hbm, latent_ref, lgain_ref, cache_ref, cos_ref, sin_ref, thr_ref, wk_ref, wv_ref,
    out_ref,
    kown, kbuf, qcbuf, qn, wq, qmsg, qbuf, q_all, wmsg, wbuf, acc, top, osend,
    wqsem, lsem, xsem, zs, zr, ys, yr, cs, cr, qs, qr, ws, wr, wxsem, fsem, os, orr,
):
    ctx = lax.axis_index("ctx")
    wt = lax.axis_index("wt")
    y = lax.axis_index("head")
    z, xl, core = ctx // 2, ctx % 2, wt % 2
    e = core * 4 + y
    partner = (ctx + 1 - 2 * xl, wt, y)
    up = ((ctx + 2) % 16, wt, y)
    down = ((ctx + 14) % 16, wt, y)
    sib = (ctx, wt + 1 - 2 * core, y)
    far_wt = (wt + 2) % 4
    far = (ctx, far_wt, y)
    yup = (ctx, wt, (y + 1) % 4)
    ydown = (ctx, wt, (y + 3) % 4)

    wq_copy = pltpu.make_async_copy(wq_hbm, wq, wqsem)
    wq_copy.start()
    barrier = pltpu.get_barrier_semaphore()
    greeted = [((ctx + i) % 16, wt, y) for i in range(1, 16)] + [yup, ydown, sib, far]
    for device in greeted:
        pl.semaphore_signal(barrier, inc=1, device_id=device, device_id_type=MESH)

    lane = lax.broadcasted_iota(jnp.int32, (32, 128), 1)

    def rotated(part, s):
        twice = jnp.concatenate([part, part], axis=1)
        return twice * cos_ref[s] + pltpu.roll(twice, 32, 1) * sin_ref[s]

    for s in range(2):
        kown[s, 0:256, 0:512] = cache_ref[s, :, 0:512]
        tail = cache_ref[s, :, 512:576]
        kown[s, 0:256, 512:640] = jnp.concatenate([tail, tail], axis=1)
        lat = latent_ref[s, :, 0:512].astype(jnp.float32)
        lat = lat * lax.rsqrt(jnp.mean(lat * lat, axis=1, keepdims=True) + eps) * lgain_ref[...]
        kown[s, 256:320, 0:512] = lat.astype(jnp.bfloat16)
        kown[s, 256:320, 512:640] = rotated(latent_ref[s, :, 512:576].astype(jnp.float32), s).astype(jnp.bfloat16)
    qcbuf[wt] = qc_ref[...].reshape(128, 384)
    wmsg[:, :, 0:128] = wk_ref[...]
    wmsg[:, :, 128:256] = wv_ref[...]
    wbuf[z, xl] = wmsg[z]
    acc[...] = jnp.zeros_like(acc)
    top[...] = jnp.full_like(top, NEG)
    pl.semaphore_wait(barrier, len(greeted))

    pending = []

    def start(copy):
        copy.start()
        pending.append(copy)

    def qc_copy(owner, idx, device):
        return remote(qcbuf.at[owner], qcbuf.at[owner], fsem.at[0, idx], fsem.at[1, idx], device)

    start(qc_copy(wt, 0, far))
    start(qc_copy(wt, 1, sib))

    rows = pl.ds(pl.multiple_of(y * SLICE, 16), SLICE)
    mine = kbuf.at[z, e]
    own_k = pltpu.make_async_copy(kown.at[xl, rows], mine, lsem)
    x_copy = remote(kown.at[1 - xl, rows], mine, xsem.at[0], xsem.at[1], partner)

    @pl.when(xl == core)
    def _():
        x_copy.start()
        own_k.start()
        own_k.wait()

    @pl.when(xl != core)
    def _():
        x_copy.wait_recv()

    first, second = pl.ds(0, CUT), pl.ds(CUT, SLICE - CUT)

    def slot(b, dy, c):
        return kbuf.at[(z + ORDER[b] + 8) % 8, c * 4 + (y + dy + 4) % 4]

    def z_copy(b, direction, idx, part=None):
        ref = slot(b, 0, core)
        if part is not None:
            ref = ref.at[part]
        return remote(ref, ref, zs.at[idx], zr.at[idx], up if direction > 0 else down)

    def y_copy(b, dy, kind, part=None):
        ref = slot(b, dy, core)
        if part is not None:
            ref = ref.at[part]
        return remote(ref, ref, ys.at[b, kind], yr.at[b, kind], yup if kind % 2 == 0 else ydown)

    def c_copy(b, kind, c):
        ref = slot(b, DY[kind], c)
        return remote(ref, ref, cs.at[b, kind], cr.at[b, kind], sib)

    def begin(b):
        start(y_copy(b, 0, 0))
        start(y_copy(b, 0, 1))
        start(c_copy(b, 0, core))

    def middle(b):
        y_copy(b, -1, 0).wait_recv()
        start(y_copy(b, -1, 2, first))
        start(c_copy(b, 1, core))
        y_copy(b, 1, 1).wait_recv()
        start(y_copy(b, 1, 3, second))
        start(c_copy(b, 2, core))

    def finish(b):
        y_copy(b, 2, 2, first).wait_recv()
        y_copy(b, 2, 3, second).wait_recv()
        start(c_copy(b, 3, core))

    def arrive(b):
        direction = 1 if b % 2 == 1 else -1
        if b == 7:
            z_copy(b, 1, 6, first).wait_recv()
            z_copy(b, -1, 7, second).wait_recv()
        else:
            z_copy(b, direction, b - 1).wait_recv()
            if b < 5:
                start(z_copy(b, direction, b + 1))
            elif direction > 0:
                start(z_copy(b, direction, 6, first))
            else:
                start(z_copy(b, direction, 7, second))
        begin(b)

    start(z_copy(0, 1, 0))
    start(z_copy(0, -1, 1))
    begin(0)

    def w_copy(i):
        dest = (z + i) % 8
        return remote(wmsg.at[dest], wbuf.at[z, xl], ws.at[i], wr.at[i], (2 * dest + xl, wt, y))

    @pl.loop(1, 8)
    def _(i):
        w_copy(i).start()

    qc_copy(far_wt, 0, far).wait_recv()
    start(qc_copy(far_wt, 2, sib))
    sib_wt = wt + 1 - 2 * core
    qc_copy(sib_wt, 1, sib).wait_recv()
    arrive(1)
    arrive(2)
    qc_copy((sib_wt + 2) % 4, 2, sib).wait_recv()

    total = jnp.zeros((128, 1), jnp.float32)
    for k in range(4):
        part = qcbuf[k].astype(jnp.float32)
        total = total + jnp.sum(part * part, axis=1, keepdims=True)
    inverse = lax.rsqrt(total * (1.0 / 1536.0) + eps)
    for k in range(4):
        cols = slice(384 * k, 384 * k + 384)
        qn[:, cols] = (qcbuf[k].astype(jnp.float32) * inverse * gain_ref[:, cols]).astype(jnp.bfloat16)
    wq_copy.wait()

    def project(k):
        full = jnp.dot(qn[...], wq[:, 384 * k : 384 * k + 384], preferred_element_type=jnp.float32)
        for a in range(2):
            for s in range(2):
                tokens = full[64 * s : 64 * s + 64]
                d = 2 * (2 * k + a) + s
                qmsg[d, 0:64] = tokens[:, 192 * a : 192 * a + 128].astype(jnp.bfloat16)
                turned = rotated(tokens[:, 192 * a + 128 : 192 * a + 192], s)
                qmsg[d, 64:96] = jnp.where(lane < 64, turned[0:32], turned[32:64]).astype(jnp.bfloat16)

    project(0)
    project(1)
    middle(0)
    project(2)
    project(3)
    qbuf[ctx] = qmsg[ctx]

    def q_copy(i):
        dest = (ctx + i) % 16
        return remote(qmsg.at[dest], qbuf.at[ctx], qs.at[i], qr.at[i], (dest, wt, y))

    @pl.loop(1, 16)
    def _(i):
        q_copy(i).start()

    @pl.loop(1, 8)
    def _(i):
        src = (z + 8 - i) % 8
        remote(wmsg.at[0], wbuf.at[src, xl], ws.at[i], wr.at[i], partner).wait_recv()

    def wx_copy(half):
        return remote(wbuf.at[:, half], wbuf.at[:, half], wxsem.at[0], wxsem.at[1], partner)

    start(wx_copy(xl))

    arrive(3)
    arrive(4)
    finish(0)
    middle(1)
    middle(2)

    @pl.loop(1, 16)
    def _(i):
        src = (ctx + 16 - i) % 16
        remote(qmsg.at[0], qbuf.at[src], qs.at[i], qr.at[i], partner).wait_recv()

    for d in range(16):
        at = 64 * d
        q_all[at : at + 64, 0:128] = qbuf[d, 0:64]
        packed = qbuf[d, 64:96]
        zero = jnp.zeros_like(packed)
        q_all[at : at + 32, 128:256] = jnp.where(lane < 64, packed, zero)
        q_all[at + 32 : at + 64, 128:256] = jnp.where(lane < 64, zero, packed)
    wx_copy(1 - xl).wait_recv()

    def o_copy(d):
        piece = pl.ds(pl.multiple_of(d * 64, 64), 64)
        return remote(osend.at[piece], out_ref.at[ctx], os.at[d], orr.at[ctx], (d, wt, y))

    def attend(b):
        for kind in range(4):
            c_copy(b, kind, 1 - core).wait_recv()
        zz = (z + ORDER[b] + 8) % 8
        block = kbuf[zz].reshape(KEYS, 640)
        weight = wbuf[...].reshape(512, 256)
        kv = jnp.dot(block[:, :512], weight, preferred_element_type=jnp.float32)
        key = jnp.concatenate([kv[:, :128].astype(jnp.bfloat16), block[:, 512:]], axis=1)
        value = jnp.concatenate([kv[:, 128:].astype(jnp.bfloat16), jnp.ones((KEYS, 128), jnp.bfloat16)], axis=1)
        threshold = thr_ref[zz]
        for g in range(4):
            g_now = (g + z // 2) % 4
            group = pl.ds(pl.multiple_of(g_now * 256, 256), 256)
            scores = lax.dot_general(
                q_all[group, :], key, (((1,), (1,)), ((), ())), preferred_element_type=jnp.float32
            )
            token = g_now * 256 + lax.broadcasted_iota(jnp.int32, (256, 1), 0)
            scores = jnp.where(token >= threshold, scores, NEG)
            old = top[group, :]
            new = jnp.maximum(old, jnp.max(scores, axis=1, keepdims=True))
            weights = jnp.exp2((scores - new[:, :1]) * SCALE).astype(jnp.bfloat16)
            shrink = jnp.exp2((old - new) * SCALE)
            top[group, :] = new
            sums = acc[group, :] * jnp.concatenate([shrink, shrink], axis=1) + jnp.dot(
                weights, value, preferred_element_type=jnp.float32
            )
            if b < 7:
                acc[group, :] = sums
            else:
                osend[group, :] = (sums[:, :128] / sums[:, 128:]).astype(jnp.bfloat16)
                for i in range(4):
                    d = g_now * 4 + i

                    @pl.when(d != ctx)
                    def _(d=d):
                        o_copy(d).start()

    attend(0)
    arrive(5)
    arrive(6)
    finish(1)
    finish(2)
    middle(3)
    middle(4)
    attend(1)
    arrive(7)
    finish(3)
    finish(4)
    middle(5)
    middle(6)
    attend(2)
    middle(7)
    finish(5)
    finish(6)
    attend(3)
    finish(7)
    attend(4)
    attend(5)
    attend(6)
    attend(7)
    out_ref[ctx] = osend[pl.ds(pl.multiple_of(ctx * 64, 64), 64), :]

    for copy in pending:
        copy.wait_send()

    @pl.when(xl == core)
    def _():
        x_copy.wait_send()

    @pl.loop(1, 8)
    def _(i):
        w_copy(i).wait_send()

    @pl.loop(1, 16)
    def _(i):
        q_copy(i).wait_send()
        other = (ctx + i) % 16
        o_copy(other).wait_send()
        remote(osend.at[pl.ds(0, 64)], out_ref.at[other], os.at[other], orr.at[other], partner).wait_recv()


def shards(
    query_compressed, query_gain, w_query, new_latent, latent_gain, cache, prefix_len, w_key_up, w_value_up
):
    ctx = lax.axis_index("ctx")
    token = ctx * 64 + jnp.arange(64, dtype=jnp.int32)
    positions = (prefix_len[:, None] + token[None, :]).astype(jnp.float32)
    frequency = jnp.exp(jnp.arange(32, dtype=jnp.float32) * (-2.0 / 64) * jnp.log(jnp.float32(rope_base)))
    angles = positions[..., None] * frequency
    cosine, sine = jnp.cos(angles), jnp.sin(angles)
    cosine = jnp.concatenate([cosine] * 4, -1)
    sine = jnp.concatenate([-sine, sine] * 2, -1)

    n = jnp.arange(8 * KEYS, dtype=jnp.int32).reshape(8, 1, KEYS)
    owner = n // (4 * SLICE)
    row = n % (4 * SLICE)
    here = jnp.sum(jnp.where(jnp.arange(2) == ctx % 2, prefix_len, 0))
    threshold = jnp.where(row < 256, jnp.where(owner * 256 + row < here, -1, 1 << 20), owner * 64 + row - 256)

    vmem = pl.BlockSpec(memory_space=pltpu.VMEM)
    any_spec = pl.BlockSpec(memory_space=pl.ANY)
    dma = pltpu.SemaphoreType.DMA
    bf16, f32 = jnp.bfloat16, jnp.float32
    out = pl.pallas_call(
        kernel,
        out_shape=jax.ShapeDtypeStruct((16, 64, 128), bf16),
        in_specs=[vmem, vmem, any_spec] + [vmem] * 8,
        out_specs=vmem,
        scratch_shapes=[
            pltpu.VMEM((2, 320, 640), bf16),
            pltpu.VMEM((8, 8, SLICE, 640), bf16),
            pltpu.VMEM((4, 128, 384), bf16),
            pltpu.VMEM((128, 1536), bf16),
            pltpu.VMEM((1536, 1536), bf16),
            pltpu.VMEM((16, 96, 128), bf16),
            pltpu.VMEM((16, 96, 128), bf16),
            pltpu.VMEM((1024, 256), bf16),
            pltpu.VMEM((8, 32, 256), bf16),
            pltpu.VMEM((8, 2, 32, 256), bf16),
            pltpu.VMEM((1024, 256), f32),
            pltpu.VMEM((1024, 128), f32),
            pltpu.VMEM((1024, 128), bf16),
            dma, dma, dma((2,)), dma((8,)), dma((8,)), dma((8, 4)), dma((8, 4)), dma((8, 4)), dma((8, 4)),
            dma((16,)), dma((16,)), dma((8,)), dma((8,)), dma((2,)), dma((2, 3)), dma((16,)), dma((16,)),
        ],
        compiler_params=pltpu.CompilerParams(
            collective_id=0, has_side_effects=True, vmem_limit_bytes=50 * 1024 * 1024
        ),
        cost_estimate=pl.CostEstimate(flops=8 * 10**9, bytes_accessed=8 * 10**6, transcendentals=5 * 10**6),
        name="attention",
    )(
        query_compressed, query_gain.reshape(1, 1536), w_query, new_latent, latent_gain.reshape(1, 512), cache,
        cosine, sine, threshold, w_key_up, w_value_up,
    )
    return jnp.transpose(out.reshape(8, 2, 64, 128), (1, 2, 0, 3)).reshape(2, 64, 1024)


def solution(mesh):
    return jax.shard_map(
        shards,
        mesh=mesh,
        in_specs=(
            P(None, "ctx", "wt"),
            P(),
            P(None, ("wt", "head")),
            P(None, "ctx", None),
            P(),
            P(None, "ctx", None),
            P(),
            P(("wt", "head"), "ctx", None),
            P(("wt", "head"), "ctx", None),
        ),
        out_specs=P(None, "ctx", ("wt", "head")),
        check_vma=False,
    )
```
